32 devices in a mesh: groups: 2 (over x), tok: 16 (over z, y, core).
Axes of the slice: x: 2, y: 2, z: 4, core: 2. Of those that a mesh axis runs over, the one named last changes fastest.
Arguments:
- key_vectors: bfloat16 [4096, 4, 2048], P(('groups', 'tok')), parts along dimension 0, may hold values from -6 to 6
- beta_values: float32 [4096, 4, 16], P(('groups', 'tok')), parts along dimension 0, may hold values from 1 to 2
- gate_decay: float32 [4096, 16], P(('groups', 'tok')), parts along dimension 0, as said below
- input_rows: bfloat16 [4096, 2048], P(('groups', 'tok')), parts along dimension 0, may hold values from -0.3125 to 0.3125
- init_state: float32 [4096], P('groups'), parts along dimension 0, may hold values from -6 to 6
- w_out: bfloat16 [2048, 2048], P(None, 'tok'), may hold values from -0.125 to 0.125
Outputs:
- states: bfloat16 [4096, 2048], P(('groups', 'tok')), parts along dimension 0
- projected: bfloat16 [4096, 2048], P(('groups', 'tok')), parts along dimension 0
The draws below stay inside these ranges and needn't reach their ends.
There are 2 independent parts, one for each index of `groups`. The reference program is written for one: setup_inputs(seed, part) draws one part's arguments, and reference() takes and returns one part's arrays. A program takes and returns all parts, laid end to end along the dimension named above; an argument that names none is the same for every part. Nothing has to cross between parts.
Inputs may be any that keep to these rules, and one draw needn't show every extreme that they name: `gate_decay`: decays are not negative.
All inputs are finite; a program needn't handle non-finite values.
Results may differ from the reference program's by a relative error of at most 0.0049.
Values may be sent and summed in bfloat16 or wider, within the bound.
A program may use at most 192 MiB of HBM per device.

```python
import math
import jax
import jax.numpy as jnp
from jax import lax

BS = 128
NB = 16
REFL = 4
DOUT = 2048
TOK_DEV = 128
S = 2048
SEQUENCE_TOKENS = 2048


def fast_blocks(key):
    share = 0.5
    return jax.random.uniform(jax.random.fold_in(key, 11), (NB,)) < share


def draw_beta_values(key, part):
    fast = fast_blocks(key)
    slow_scale = jnp.exp(jax.random.uniform(jax.random.fold_in(key, 12), (NB,), minval=math.log(1e-05), maxval=math.log(0.0003)))
    fast_scale = jax.random.uniform(jax.random.fold_in(key, 13), (NB,), minval=0.3, maxval=1.0)
    block_scale = jnp.where(fast, fast_scale, slow_scale)
    spread = jax.random.uniform(jax.random.fold_in(key, 14), (SEQUENCE_TOKENS, REFL, NB), minval=0.05, maxval=1.0)
    return (2.0 - block_scale[None, None, :] * spread).astype(jnp.float32)


def draw_gate_decay(key, part):
    fast = fast_blocks(key)
    fast_rate = jax.random.uniform(jax.random.fold_in(key, 15), (NB,), minval=1.0 / 50.0, maxval=1.0 / 30.0)
    slow_rate = jnp.exp(jax.random.uniform(jax.random.fold_in(key, 16), (NB,), minval=math.log(1e-05), maxval=math.log(4e-05)))
    baseline_rate = jnp.where(fast, fast_rate, slow_rate)
    device_factor = jnp.exp(jax.random.uniform(jax.random.fold_in(key, 17), (SEQUENCE_TOKENS // TOK_DEV,), minval=-0.7, maxval=0.7))
    rows_per_device = jnp.repeat(device_factor, TOK_DEV, total_repeat_length=SEQUENCE_TOKENS)
    jaggedness = jax.random.uniform(jax.random.fold_in(key, 18), (SEQUENCE_TOKENS, NB), minval=0.5, maxval=1.5)
    spike_position = jax.random.randint(jax.random.fold_in(key, 19), (3,), 0, SEQUENCE_TOKENS)
    spike_length = jax.random.uniform(jax.random.fold_in(key, 20), (3,), minval=0.22, maxval=0.69)
    arrival_count = (jnp.arange(SEQUENCE_TOKENS)[:, None] == spike_position[None, :]).astype(jnp.float32)
    sudden_spike = jnp.sum(arrival_count * spike_length[None, :], axis=1)
    return (rows_per_device[:, None] * jaggedness * baseline_rate[None, :] + sudden_spike[:, None]).astype(jnp.float32)


def shard_levels(stream_key, extent, split, least, largest):
    def one(dim, parts):
        heights = jax.random.uniform(jax.random.fold_in(jax.random.fold_in(stream_key, 6), dim), (parts,), jnp.float32, least / len(split), largest / len(split))
        return jnp.repeat(jnp.exp(heights), extent[dim] // parts).reshape((-1,) + (1,) * (len(extent) - dim - 1))

    loudness = one(*split[0])
    for cut in split[1:]:
        loudness = loudness * one(*cut)
    return loudness


def scatter_about(key, shape, scale, most, cuts=(), held_as=jnp.bfloat16):
    factor_of = shard_levels(key, shape, cuts, -0.22, 0.18) if cuts else 1.0
    array = jax.random.normal(key, shape, jnp.float32) * scale * factor_of
    return jnp.minimum(jnp.maximum(array, -most), most).astype(held_as)


def setup_inputs(seed: int = 0, part: int = 0) -> dict:
    keys = jax.random.split(jax.random.key(seed), 7)
    part_keys = jax.random.split(jax.random.fold_in(keys[6], part), 7)
    key_vectors = scatter_about(part_keys[0], (SEQUENCE_TOKENS, REFL, S), 1.0, 6.0, ((0, 16),))
    beta_values = draw_beta_values(jax.random.fold_in(jax.random.fold_in(keys[6], part), 71), part)
    gate_decay = draw_gate_decay(jax.random.fold_in(jax.random.fold_in(keys[6], part), 71), part)
    input_rows = scatter_about(part_keys[3], (SEQUENCE_TOKENS, S), 0.02, 0.3125, ((0, 16),))
    init_state = scatter_about(part_keys[4], (S,), 1.0, 6.0, (), jnp.float32)
    w_out = scatter_about(keys[5], (S, DOUT), S ** -0.5, 0.125, ((1, 16),))
    return {"key_vectors": key_vectors, "beta_values": beta_values, "gate_decay": gate_decay, "input_rows": input_rows, "init_state": init_state, "w_out": w_out}


epsilon = 1e-06

def reference(key_vectors, beta_values, gate_decay, input_rows, init_state, w_out):
    state_width = key_vectors.shape[2]
    blocks = state_width // BS

    def advance(current, pieces):
        key_rows, strength, decay_rows, feed_row = pieces
        raw_keys = key_rows.astype(jnp.float32).reshape(REFL, blocks, BS)
        unit_keys = raw_keys * lax.rsqrt(lax.optimization_barrier(jnp.sum(raw_keys * raw_keys, axis=-1, keepdims=True)) + epsilon)
        current = current * jnp.exp(-decay_rows)[:, None]
        for reflection in range(REFL):
            along_keys = lax.optimization_barrier(jnp.sum(unit_keys[reflection] * current, axis=-1, keepdims=True))
            current = current - strength[reflection][:, None] * unit_keys[reflection] * along_keys
        current = current + feed_row.astype(jnp.float32).reshape(blocks, BS)
        return (current, current.reshape(state_width).astype(jnp.bfloat16))
    _, states = lax.scan(advance, init_state.reshape(blocks, BS), (key_vectors, beta_values, gate_decay, input_rows))
    projected = jnp.dot(states, w_out, preferred_element_type=jnp.float32).astype(jnp.bfloat16)
    return (states, projected)
```

```python
import functools
import jax
import jax.numpy as jnp
from jax import lax
from jax.experimental import pallas as pl
from jax.experimental.pallas import tpu as pltpu
from jax.sharding import PartitionSpec as P

BS = 128
REFL = 4
WIN = BS // REFL
epsilon = 1e-06
F32 = jnp.float32
BF16 = jnp.bfloat16


def iota(shape, dim):
    return lax.broadcasted_iota(jnp.int32, shape, dim)


def split(a):
    high = a.astype(BF16)
    return high, (a - high.astype(F32)).astype(BF16)


def dot(a, b, dims=((1,), (0,))):
    return lax.dot_general(a, b, (dims, ((), ())), preferred_element_type=F32)


def dot3(a, b):
    (ah, al), (bh, bl) = a, b
    return dot(jnp.concatenate([ah, al, ah], 1), jnp.concatenate([bh, bh, bl], 0))


def to_col(row, eye):
    return jnp.sum(jnp.where(eye, row, 0.0), axis=1, keepdims=True)


def to_row(col, eye):
    return jnp.sum(jnp.where(eye, col, 0.0), axis=0, keepdims=True)


def local_kernel(per, windows, k_ref, vec_ref, v_ref, map_ref, end_ref, z_ref, z0_ref):
    i, j = iota((BS, BS), 0), iota((BS, BS), 1)
    eye = i == j
    eye_f = eye.astype(F32)
    tok, refl = iota((WIN, BS), 0), iota((WIN, BS), 1)
    systems = [(b, w) for b in range(per) for w in range(windows)]

    keys = {}
    a_mats, col_q, push, cums = {}, {}, {}, {}
    for b, w in systems:
        k = k_ref[w * BS : (w + 1) * BS, b * BS : (b + 1) * BS]
        v = v_ref[w * WIN : (w + 1) * WIN, b * BS : (b + 1) * BS]
        beta = vec_ref[b, w : w + 1, :]
        cum = vec_ref[b, windows + w : windows + w + 1, :]
        cum_col = to_col(cum, eye)
        tok_col = jnp.sum(jnp.where(refl == REFL * tok, cum, 0.0), axis=1, keepdims=True)
        gram = dot(k, k, ((1,), (1,)))
        q_row = beta / (to_row(gram, eye) + epsilon)
        q_col = to_col(q_row, eye)
        a_mats[b, w] = jnp.where(
            j < i, q_col * jnp.exp(jnp.minimum(cum - cum_col, 0.0)) * gram, 0.0
        )
        feed = dot(v, k, ((1,), (1,)))
        weigh = jnp.where(
            tok < refl // REFL, jnp.exp(jnp.minimum(tok_col - cum, 0.0)) * feed, 0.0
        )
        push[b, w] = q_row * jnp.sum(weigh, axis=0, keepdims=True)
        keys[b, w] = k
        col_q[b, w] = q_row * jnp.exp(-cum)
        cums[b, w] = (cum, cum_col, tok_col)

    inv = {s: jnp.where(eye, 1.0, jnp.where((i // 2 == j // 2), -a_mats[s], 0.0)) for s in systems}
    size = 2
    while size < BS:
        below = (i // (2 * size) == j // (2 * size)) & (i // size != j // size)
        for s in systems:
            t = split(inv[s])
            x = dot3(split(jnp.where(below, a_mats[s], 0.0)), t)
            inv[s] = inv[s] - dot3(t, split(x))
        size *= 2

    maps, ends = {}, {}
    for b, w in systems:
        s = (b, w)
        k = keys[s]
        cum, cum_col, tok_col = cums[s]
        cum_end = cum[:, BS - 1 : BS]
        th, tl = split(inv[s] * col_q[s])
        z = dot(jnp.concatenate([th, tl], 1), jnp.concatenate([k, k], 0))
        z0 = jnp.sum(inv[s] * push[s], axis=1, keepdims=True)
        z_ref[b, w] = z
        z0_ref[b, w : w + 1, :] = to_row(z0, eye)
        to_end = jnp.exp(cum_col - cum_end)
        eh, el = split(to_end * z)
        maps[s] = jnp.exp(-cum_end) * eye_f - dot(
            jnp.concatenate([eh, el], 0), jnp.concatenate([k, k], 0), ((0,), (0,))
        )
        v = v_ref[w * WIN : (w + 1) * WIN, b * BS : (b + 1) * BS].astype(F32)
        ends[s] = jnp.sum(jnp.exp(tok_col - cum_end) * v, axis=0, keepdims=True) - jnp.sum(
            (to_end * z0) * k.astype(F32), axis=0, keepdims=True
        )

    for b in range(per):
        end = ends[b, 0]
        total = maps[b, 0]
        for w in range(1, windows):
            end = jnp.sum(to_col(end, eye) * maps[b, w], axis=0, keepdims=True) + ends[b, w]
            total = dot3(split(total), split(maps[b, w]))
        map_ref[b] = total
        end_ref[b] = end


def chain_kernel(axis, map_ref, end_ref, init_ref, out_ref, held, going, send_sem, recv_sem):
    blocks = init_ref.shape[0]
    count, me = lax.axis_size(axis), lax.axis_index(axis)
    first, last = me == 0, me == count - 1
    barrier = pltpu.get_barrier_semaphore()

    @pl.when(jnp.logical_not(first))
    def _():
        pl.semaphore_signal(
            barrier, inc=1, device_id={axis: me - 1}, device_id_type=pl.DeviceIdType.MESH
        )

    @pl.when(jnp.logical_not(last))
    def _():
        pl.semaphore_signal(
            barrier, inc=1, device_id={axis: me + 1}, device_id_type=pl.DeviceIdType.MESH
        )

    pl.semaphore_wait(
        barrier, jnp.where(first, 0, 1).astype(jnp.int32) + jnp.where(last, 0, 1).astype(jnp.int32)
    )

    def copy(to):
        return pltpu.make_async_remote_copy(
            src_ref=going,
            dst_ref=held,
            send_sem=send_sem,
            recv_sem=recv_sem,
            device_id={axis: to},
            device_id_type=pl.DeviceIdType.MESH,
        )

    @pl.when(first)
    def _():
        out_ref[...] = init_ref[...]

    @pl.when(jnp.logical_not(first))
    def _():
        copy(lax.rem(me + 1, count)).wait_recv()
        out_ref[...] = held[...]

    @pl.when(jnp.logical_not(last))
    def _():
        columns = out_ref[...].T
        for b in range(blocks):
            going[b : b + 1, :] = (
                jnp.sum(columns[:, b : b + 1] * map_ref[b], axis=0, keepdims=True) + end_ref[b]
            )
        sending = copy(me + 1)
        sending.start()
        sending.wait_send()


def finish_kernel(per, windows, k_ref, vec_ref, v_ref, z_ref, z0_ref, x_ref, w_ref, s_ref, p_ref, acc):
    step = pl.program_id(0)
    eye = iota((BS, BS), 0) == iota((BS, BS), 1)
    tok, refl = iota((WIN, BS), 0), iota((WIN, BS), 1)
    ti, tj = iota((WIN, WIN), 0), iota((WIN, WIN), 1)
    now = [x_ref[b] for b in range(per)]
    for w in range(windows):
        for b in range(per):
            x = now[b]
            k = k_ref[w * BS : (w + 1) * BS, b * BS : (b + 1) * BS]
            v = v_ref[w * WIN : (w + 1) * WIN, b * BS : (b + 1) * BS]
            cum = vec_ref[b, windows + w : windows + w + 1, :]
            tok_col = jnp.sum(jnp.where(refl == REFL * tok, cum, 0.0), axis=1, keepdims=True)
            tok_row = to_row(tok_col, ti == tj)
            z = to_row(jnp.sum(z_ref[b, w] * x, axis=1, keepdims=True), eye) + z0_ref[b, w : w + 1, :]
            take = jnp.where(
                refl // REFL <= tok, jnp.exp(jnp.minimum(cum - tok_col, 0.0)) * z, 0.0
            )
            give = jnp.where(tj <= ti, jnp.exp(jnp.minimum(tok_row - tok_col, 0.0)), 0.0)
            th, tl = split(take)
            gh, gl = split(give)
            rows = (
                jnp.exp(-tok_col) * x
                + (dot(gh, v) + dot(gl, v))
                - dot(jnp.concatenate([th, tl], 1), jnp.concatenate([k, k], 0))
            )
            s_ref[w * WIN : (w + 1) * WIN, b * BS : (b + 1) * BS] = rows.astype(BF16)
            now[b] = rows[WIN - 1 : WIN, :]
    part = dot(s_ref[...], w_ref[...])

    @pl.when(step == 0)
    def _():
        acc[...] = part

    @pl.when(step > 0)
    def _():
        acc[...] += part

    @pl.when(step == pl.num_programs(0) - 1)
    def _():
        p_ref[...] = acc[...].astype(BF16)


def shards(key_vectors, beta_values, gate_decay, input_rows, init_state, w_out):
    tok_rows, _, width = key_vectors.shape
    blocks = width // BS
    windows = tok_rows // WIN
    refl_rows = REFL * tok_rows
    per = 2
    keys = key_vectors.reshape(refl_rows, width)
    pos = jnp.arange(WIN)
    up_to = (pos[None, :] <= pos[:, None]).astype(F32)
    cum = jnp.einsum(
        "ts,csb->bct", up_to, gate_decay.reshape(windows, WIN, blocks), precision=lax.Precision.HIGHEST
    )
    vec = jnp.concatenate(
        [
            beta_values.reshape(windows, BS, blocks).transpose(2, 0, 1),
            jnp.repeat(cum, REFL, axis=2),
        ],
        axis=1,
    )
    full_w = lax.all_gather(w_out, "tok", axis=1, tiled=True)
    vmem = 48 * 1024 * 1024
    key_spec = pl.BlockSpec((refl_rows, per * BS), lambda g: (0, g))
    vec_spec = pl.BlockSpec((per, 2 * windows, BS), lambda g: (g, 0, 0))
    row_spec = pl.BlockSpec((tok_rows, per * BS), lambda g: (0, g))
    z_spec = pl.BlockSpec((per, windows, BS, BS), lambda g: (g, 0, 0, 0))
    z0_spec = pl.BlockSpec((per, windows, BS), lambda g: (g, 0, 0))
    vector_spec = pl.BlockSpec((per, 1, BS), lambda g: (g, 0, 0))
    maps, ends, z, z0 = pl.pallas_call(
        functools.partial(local_kernel, per, windows),
        grid=(blocks // per,),
        in_specs=[key_spec, vec_spec, row_spec],
        out_specs=[pl.BlockSpec((per, BS, BS), lambda g: (g, 0, 0)), vector_spec, z_spec, z0_spec],
        out_shape=[
            jax.ShapeDtypeStruct((blocks, BS, BS), F32),
            jax.ShapeDtypeStruct((blocks, 1, BS), F32),
            jax.ShapeDtypeStruct((blocks, windows, BS, BS), F32),
            jax.ShapeDtypeStruct((blocks, windows, BS), F32),
        ],
        compiler_params=pltpu.CompilerParams(vmem_limit_bytes=vmem),
        cost_estimate=pl.CostEstimate(
            flops=blocks * windows * 45 * 2 * BS**3, bytes_accessed=10 << 20, transcendentals=0
        ),
        name="local",
    )(keys, vec, input_rows)
    whole = pl.BlockSpec(memory_space=pltpu.VMEM)
    entry = pl.pallas_call(
        functools.partial(chain_kernel, "tok"),
        in_specs=[whole] * 3,
        out_specs=whole,
        out_shape=jax.ShapeDtypeStruct((blocks, BS), F32),
        scratch_shapes=[
            pltpu.VMEM((blocks, BS), F32),
            pltpu.VMEM((blocks, BS), F32),
            pltpu.SemaphoreType.DMA,
            pltpu.SemaphoreType.DMA,
        ],
        compiler_params=pltpu.CompilerParams(
            collective_id=0, has_side_effects=True, vmem_limit_bytes=vmem
        ),
        cost_estimate=pl.CostEstimate(flops=60_000_000, bytes_accessed=60 << 20, transcendentals=0),
        name="chain",
    )(maps, ends, init_state.reshape(blocks, BS))
    out = w_out.shape[1] * lax.axis_size("tok")
    states, projected = pl.pallas_call(
        functools.partial(finish_kernel, per, windows),
        grid=(blocks // per,),
        in_specs=[
            key_spec,
            vec_spec,
            row_spec,
            z_spec,
            z0_spec,
            vector_spec,
            pl.BlockSpec((per * BS, out), lambda g: (g, 0)),
        ],
        out_specs=[row_spec, pl.BlockSpec((tok_rows, out), lambda g: (0, 0))],
        out_shape=[
            jax.ShapeDtypeStruct((tok_rows, width), BF16),
            jax.ShapeDtypeStruct((tok_rows, out), BF16),
        ],
        scratch_shapes=[pltpu.VMEM((tok_rows, out), F32)],
        compiler_params=pltpu.CompilerParams(vmem_limit_bytes=vmem),
        name="finish",
    )(keys, vec, input_rows, z, z0, entry.reshape(blocks, 1, BS), full_w)
    return (states, projected)


def solution(mesh):
    return jax.shard_map(
        shards,
        mesh=mesh,
        in_specs=(
            P(("groups", "tok"), None, None),
            P(("groups", "tok"), None, None),
            P(("groups", "tok"), None),
            P(("groups", "tok"), None),
            P("groups"),
            P(None, "tok"),
        ),
        out_specs=(P(("groups", "tok"), None), P(("groups", "tok"), None)),
        check_vma=False,
    )
```

```python
import functools
import jax
import jax.numpy as jnp
from jax import lax
from jax.experimental import pallas as pl
from jax.experimental.pallas import tpu as pltpu
from jax.sharding import PartitionSpec as P

BS = 128
REFL = 4
WIN = BS // REFL
epsilon = 1e-06
F32 = jnp.float32
BF16 = jnp.bfloat16


def iota(shape, dim):
    return lax.broadcasted_iota(jnp.int32, shape, dim)


def split(a):
    high = a.astype(BF16)
    return high, (a - high.astype(F32)).astype(BF16)


def dot(a, b, dims=((1,), (0,))):
    return lax.dot_general(a, b, (dims, ((), ())), preferred_element_type=F32)


def dot3(a, b):
    (ah, al), (bh, bl) = a, b
    return dot(ah, bh) + (dot(al, bh) + dot(ah, bl))


def to_col(row, eye):
    return jnp.sum(jnp.where(eye, row, 0.0), axis=1, keepdims=True)


def to_row(col, eye):
    return jnp.sum(jnp.where(eye, col, 0.0), axis=0, keepdims=True)


def local_kernel(per, windows, k_ref, vec_ref, v_ref, map_ref, end_ref, z_ref, z0_ref):
    i, j = iota((BS, BS), 0), iota((BS, BS), 1)
    eye = i == j
    eye_f = eye.astype(F32)
    tok, refl = iota((WIN, BS), 0), iota((WIN, BS), 1)
    systems = [(b, w) for b in range(per) for w in range(windows)]

    keys = {}
    a_mats, col_q, push, cums = {}, {}, {}, {}
    for b, w in systems:
        k = k_ref[w * BS : (w + 1) * BS, b * BS : (b + 1) * BS]
        v = v_ref[w * WIN : (w + 1) * WIN, b * BS : (b + 1) * BS]
        beta = vec_ref[b, w : w + 1, :]
        cum = vec_ref[b, windows + w : windows + w + 1, :]
        cum_col = to_col(cum, eye)
        tok_col = jnp.sum(jnp.where(refl == REFL * tok, cum, 0.0), axis=1, keepdims=True)
        gram = dot(k, k, ((1,), (1,)))
        q_row = beta / (to_row(gram, eye) + epsilon)
        q_col = to_col(q_row, eye)
        a_mats[b, w] = jnp.where(
            j < i, q_col * jnp.exp(jnp.minimum(cum - cum_col, 0.0)) * gram, 0.0
        )
        feed = dot(v, k, ((1,), (1,)))
        weigh = jnp.where(
            tok < refl // REFL, jnp.exp(jnp.minimum(tok_col - cum, 0.0)) * feed, 0.0
        )
        push[b, w] = q_row * jnp.sum(weigh, axis=0, keepdims=True)
        keys[b, w] = k
        col_q[b, w] = q_row * jnp.exp(-cum)
        cums[b, w] = (cum, cum_col, tok_col)

    inv = {s: jnp.where(eye, 1.0, jnp.where((i // 2 == j // 2), -a_mats[s], 0.0)) for s in systems}
    size = 2
    while size < BS:
        below = (i // (2 * size) == j // (2 * size)) & (i // size != j // size)
        for s in systems:
            t = split(inv[s])
            x = dot3(split(jnp.where(below, a_mats[s], 0.0)), t)
            inv[s] = inv[s] - dot3(t, split(x))
        size *= 2

    maps, ends = {}, {}
    for b, w in systems:
        s = (b, w)
        k = keys[s]
        cum, cum_col, tok_col = cums[s]
        cum_end = cum[:, BS - 1 : BS]
        th, tl = split(inv[s] * col_q[s])
        z = (dot(th, k) + dot(tl, k))
        z0 = jnp.sum(inv[s] * push[s], axis=1, keepdims=True)
        z_ref[b, w] = z
        z0_ref[b, w : w + 1, :] = to_row(z0, eye)
        to_end = jnp.exp(cum_col - cum_end)
        eh, el = split(to_end * z)
        maps[s] = jnp.exp(-cum_end) * eye_f - (
            dot(eh, k, ((0,), (0,))) + dot(el, k, ((0,), (0,)))
        )
        v = v_ref[w * WIN : (w + 1) * WIN, b * BS : (b + 1) * BS].astype(F32)
        ends[s] = jnp.sum(jnp.exp(tok_col - cum_end) * v, axis=0, keepdims=True) - jnp.sum(
            (to_end * z0) * k.astype(F32), axis=0, keepdims=True
        )

    for b in range(per):
        end = ends[b, 0]
        total = maps[b, 0]
        for w in range(1, windows):
            end = jnp.sum(to_col(end, eye) * maps[b, w], axis=0, keepdims=True) + ends[b, w]
            total = dot3(split(total), split(maps[b, w]))
        map_ref[b] = total
        end_ref[b] = end


def chain_kernel(axis, map_ref, end_ref, init_ref, out_ref, held, going, send_sem, recv_sem):
    blocks = init_ref.shape[0]
    count, me = lax.axis_size(axis), lax.axis_index(axis)
    first, last = me == 0, me == count - 1
    barrier = pltpu.get_barrier_semaphore()

    @pl.when(jnp.logical_not(first))
    def _():
        pl.semaphore_signal(
            barrier, inc=1, device_id={axis: me - 1}, device_id_type=pl.DeviceIdType.MESH
        )

    @pl.when(jnp.logical_not(last))
    def _():
        pl.semaphore_signal(
            barrier, inc=1, device_id={axis: me + 1}, device_id_type=pl.DeviceIdType.MESH
        )

    pl.semaphore_wait(
        barrier, jnp.where(first, 0, 1).astype(jnp.int32) + jnp.where(last, 0, 1).astype(jnp.int32)
    )

    def copy(to):
        return pltpu.make_async_remote_copy(
            src_ref=going,
            dst_ref=held,
            send_sem=send_sem,
            recv_sem=recv_sem,
            device_id={axis: to},
            device_id_type=pl.DeviceIdType.MESH,
        )

    @pl.when(first)
    def _():
        out_ref[...] = init_ref[...]

    @pl.when(jnp.logical_not(first))
    def _():
        copy(lax.rem(me + 1, count)).wait_recv()
        out_ref[...] = held[...]

    @pl.when(jnp.logical_not(last))
    def _():
        columns = out_ref[...].T
        for b in range(blocks):
            going[b : b + 1, :] = (
                jnp.sum(columns[:, b : b + 1] * map_ref[b], axis=0, keepdims=True) + end_ref[b]
            )
        sending = copy(me + 1)
        sending.start()
        sending.wait_send()


def finish_kernel(per, windows, k_ref, vec_ref, v_ref, z_ref, z0_ref, x_ref, w_ref, s_ref, p_ref, acc):
    step = pl.program_id(0)
    eye = iota((BS, BS), 0) == iota((BS, BS), 1)
    tok, refl = iota((WIN, BS), 0), iota((WIN, BS), 1)
    ti, tj = iota((WIN, WIN), 0), iota((WIN, WIN), 1)
    now = [x_ref[b] for b in range(per)]
    for w in range(windows):
        for b in range(per):
            x = now[b]
            k = k_ref[w * BS : (w + 1) * BS, b * BS : (b + 1) * BS]
            v = v_ref[w * WIN : (w + 1) * WIN, b * BS : (b + 1) * BS]
            cum = vec_ref[b, windows + w : windows + w + 1, :]
            tok_col = jnp.sum(jnp.where(refl == REFL * tok, cum, 0.0), axis=1, keepdims=True)
            tok_row = to_row(tok_col, ti == tj)
            z = to_row(jnp.sum(z_ref[b, w] * x, axis=1, keepdims=True), eye) + z0_ref[b, w : w + 1, :]
            take = jnp.where(
                refl // REFL <= tok, jnp.exp(jnp.minimum(cum - tok_col, 0.0)) * z, 0.0
            )
            give = jnp.where(tj <= ti, jnp.exp(jnp.minimum(tok_row - tok_col, 0.0)), 0.0)
            th, tl = split(take)
            gh, gl = split(give)
            rows = (
                jnp.exp(-tok_col) * x
                + (dot(gh, v) + dot(gl, v))
                - (dot(th, k) + dot(tl, k))
            )
            s_ref[w * WIN : (w + 1) * WIN, b * BS : (b + 1) * BS] = rows.astype(BF16)
            now[b] = rows[WIN - 1 : WIN, :]
    part = dot(s_ref[...], w_ref[...])

    @pl.when(step == 0)
    def _():
        acc[...] = part

    @pl.when(step > 0)
    def _():
        acc[...] += part

    @pl.when(step == pl.num_programs(0) - 1)
    def _():
        p_ref[...] = acc[...].astype(BF16)


def shards(key_vectors, beta_values, gate_decay, input_rows, init_state, w_out):
    tok_rows, _, width = key_vectors.shape
    blocks = width // BS
    windows = tok_rows // WIN
    refl_rows = REFL * tok_rows
    per = 2
    keys = key_vectors.reshape(refl_rows, width)
    pos = jnp.arange(WIN)
    up_to = (pos[None, :] <= pos[:, None]).astype(F32)
    cum = jnp.einsum(
        "ts,csb->bct", up_to, gate_decay.reshape(windows, WIN, blocks), precision=lax.Precision.HIGHEST
    )
    vec = jnp.concatenate(
        [
            beta_values.reshape(windows, BS, blocks).transpose(2, 0, 1),
            jnp.repeat(cum, REFL, axis=2),
        ],
        axis=1,
    )
    full_w = lax.all_gather(w_out, "tok", axis=1, tiled=True)
    vmem = 48 * 1024 * 1024
    key_spec = pl.BlockSpec((refl_rows, per * BS), lambda g: (0, g))
    vec_spec = pl.BlockSpec((per, 2 * windows, BS), lambda g: (g, 0, 0))
    row_spec = pl.BlockSpec((tok_rows, per * BS), lambda g: (0, g))
    z_spec = pl.BlockSpec((per, windows, BS, BS), lambda g: (g, 0, 0, 0))
    z0_spec = pl.BlockSpec((per, windows, BS), lambda g: (g, 0, 0))
    vector_spec = pl.BlockSpec((per, 1, BS), lambda g: (g, 0, 0))
    maps, ends, z, z0 = pl.pallas_call(
        functools.partial(local_kernel, per, windows),
        grid=(blocks // per,),
        in_specs=[key_spec, vec_spec, row_spec],
        out_specs=[pl.BlockSpec((per, BS, BS), lambda g: (g, 0, 0)), vector_spec, z_spec, z0_spec],
        out_shape=[
            jax.ShapeDtypeStruct((blocks, BS, BS), F32),
            jax.ShapeDtypeStruct((blocks, 1, BS), F32),
            jax.ShapeDtypeStruct((blocks, windows, BS, BS), F32),
            jax.ShapeDtypeStruct((blocks, windows, BS), F32),
        ],
        compiler_params=pltpu.CompilerParams(vmem_limit_bytes=vmem),
        cost_estimate=pl.CostEstimate(
            flops=blocks * windows * 45 * 2 * BS**3, bytes_accessed=10 << 20, transcendentals=0
        ),
        name="local",
    )(keys, vec, input_rows)
    whole = pl.BlockSpec(memory_space=pltpu.VMEM)
    entry = pl.pallas_call(
        functools.partial(chain_kernel, "tok"),
        in_specs=[whole] * 3,
        out_specs=whole,
        out_shape=jax.ShapeDtypeStruct((blocks, BS), F32),
        scratch_shapes=[
            pltpu.VMEM((blocks, BS), F32),
            pltpu.VMEM((blocks, BS), F32),
            pltpu.SemaphoreType.DMA,
            pltpu.SemaphoreType.DMA,
        ],
        compiler_params=pltpu.CompilerParams(
            collective_id=0, has_side_effects=True, vmem_limit_bytes=vmem
        ),
        cost_estimate=pl.CostEstimate(flops=60_000_000, bytes_accessed=60 << 20, transcendentals=0),
        name="chain",
    )(maps, ends, init_state.reshape(blocks, BS))
    out = w_out.shape[1] * lax.axis_size("tok")
    states, projected = pl.pallas_call(
        functools.partial(finish_kernel, per, windows),
        grid=(blocks // per,),
        in_specs=[
            key_spec,
            vec_spec,
            row_spec,
            z_spec,
            z0_spec,
            vector_spec,
            pl.BlockSpec((per * BS, out), lambda g: (g, 0)),
        ],
        out_specs=[row_spec, pl.BlockSpec((tok_rows, out), lambda g: (0, 0))],
        out_shape=[
            jax.ShapeDtypeStruct((tok_rows, width), BF16),
            jax.ShapeDtypeStruct((tok_rows, out), BF16),
        ],
        scratch_shapes=[pltpu.VMEM((tok_rows, out), F32)],
        compiler_params=pltpu.CompilerParams(vmem_limit_bytes=vmem),
        name="finish",
    )(keys, vec, input_rows, z, z0, entry.reshape(blocks, 1, BS), full_w)
    return (states, projected)


def solution(mesh):
    return jax.shard_map(
        shards,
        mesh=mesh,
        in_specs=(
            P(("groups", "tok"), None, None),
            P(("groups", "tok"), None, None),
            P(("groups", "tok"), None),
            P(("groups", "tok"), None),
            P("groups"),
            P(None, "tok"),
        ),
        out_specs=(P(("groups", "tok"), None), P(("groups", "tok"), None)),
        check_vma=False,
    )
```

```python
import functools
import jax
import jax.numpy as jnp
from jax import lax
from jax.experimental import pallas as pl
from jax.experimental.pallas import tpu as pltpu
from jax.sharding import PartitionSpec as P

BS = 128
REFL = 4
WIN = BS // REFL
epsilon = 1e-06
F32 = jnp.float32
BF16 = jnp.bfloat16


def iota(shape, dim):
    return lax.broadcasted_iota(jnp.int32, shape, dim)


def split(a):
    high = a.astype(BF16)
    return high, (a - high.astype(F32)).astype(BF16)


def dot(a, b, dims=((1,), (0,))):
    return lax.dot_general(a, b, (dims, ((), ())), preferred_element_type=F32)


def dot3(a, b):
    (ah, al), (bh, bl) = a, b
    return dot(ah, bh) + (dot(al, bh) + dot(ah, bl))


def to_col(row, eye):
    return jnp.sum(jnp.where(eye, row, 0.0), axis=1, keepdims=True)


def to_row(col, eye):
    return jnp.sum(jnp.where(eye, col, 0.0), axis=0, keepdims=True)


def local_kernel(per, windows, k_ref, vec_ref, v_ref, map_ref, end_ref, z_ref, z0_ref):
    i, j = iota((BS, BS), 0), iota((BS, BS), 1)
    eye = i == j
    eye_f = eye.astype(F32)
    tok, refl = iota((WIN, BS), 0), iota((WIN, BS), 1)
    systems = [(b, w) for b in range(per) for w in range(windows)]

    keys = {}
    a_mats, col_q, push, cums = {}, {}, {}, {}
    for b, w in systems:
        k = k_ref[w * BS : (w + 1) * BS, b * BS : (b + 1) * BS]
        v = v_ref[w * WIN : (w + 1) * WIN, b * BS : (b + 1) * BS]
        beta = vec_ref[b, w : w + 1, :]
        cum = vec_ref[b, windows + w : windows + w + 1, :]
        cum_col = to_col(cum, eye)
        tok_col = jnp.sum(jnp.where(refl == REFL * tok, cum, 0.0), axis=1, keepdims=True)
        gram = dot(k, k, ((1,), (1,)))
        q_row = beta / (to_row(gram, eye) + epsilon)
        q_col = to_col(q_row, eye)
        a_mats[b, w] = jnp.where(
            j < i, q_col * jnp.exp(jnp.minimum(cum - cum_col, 0.0)) * gram, 0.0
        )
        feed = dot(v, k, ((1,), (1,)))
        weigh = jnp.where(
            tok < refl // REFL, jnp.exp(jnp.minimum(tok_col - cum, 0.0)) * feed, 0.0
        )
        push[b, w] = q_row * jnp.sum(weigh, axis=0, keepdims=True)
        keys[b, w] = k
        col_q[b, w] = q_row * jnp.exp(-cum)
        cums[b, w] = (cum, cum_col, tok_col)

    inv = {s: jnp.where(eye, 1.0, jnp.where((i // 2 == j // 2), -a_mats[s], 0.0)) for s in systems}
    size = 2
    while size < BS:
        below = (i // (2 * size) == j // (2 * size)) & (i // size != j // size)
        for s in systems:
            t = split(inv[s])
            x = dot3(split(jnp.where(below, a_mats[s], 0.0)), t)
            inv[s] = inv[s] - dot3(t, split(x))
        size *= 2

    maps, ends = {}, {}
    for b, w in systems:
        s = (b, w)
        k = keys[s]
        cum, cum_col, tok_col = cums[s]
        cum_end = cum[:, BS - 1 : BS]
        th, tl = split(inv[s] * col_q[s])
        z = (dot(th, k) + dot(tl, k))
        z0 = jnp.sum(inv[s] * push[s], axis=1, keepdims=True)
        z_ref[b, w] = z
        z0_ref[b, w : w + 1, :] = to_row(z0, eye)
        to_end = jnp.exp(cum_col - cum_end)
        eh, el = split(to_end * z)
        maps[s] = jnp.exp(-cum_end) * eye_f - (
            dot(eh, k, ((0,), (0,))) + dot(el, k, ((0,), (0,)))
        )
        v = v_ref[w * WIN : (w + 1) * WIN, b * BS : (b + 1) * BS].astype(F32)
        ends[s] = jnp.sum(jnp.exp(tok_col - cum_end) * v, axis=0, keepdims=True) - jnp.sum(
            (to_end * z0) * k.astype(F32), axis=0, keepdims=True
        )

    for b in range(per):
        end = ends[b, 0]
        total = maps[b, 0]
        for w in range(1, windows):
            end = jnp.sum(to_col(end, eye) * maps[b, w], axis=0, keepdims=True) + ends[b, w]
            total = dot3(split(total), split(maps[b, w]))
        map_ref[b] = total
        end_ref[b] = end


def chain_kernel(axis, map_ref, end_ref, init_ref, out_ref, held, going, send_sem, recv_sem):
    blocks = init_ref.shape[0]
    count, me = lax.axis_size(axis), lax.axis_index(axis)
    first, last = me == 0, me == count - 1
    barrier = pltpu.get_barrier_semaphore()

    @pl.when(jnp.logical_not(first))
    def _():
        pl.semaphore_signal(
            barrier, inc=1, device_id={axis: me - 1}, device_id_type=pl.DeviceIdType.MESH
        )

    @pl.when(jnp.logical_not(last))
    def _():
        pl.semaphore_signal(
            barrier, inc=1, device_id={axis: me + 1}, device_id_type=pl.DeviceIdType.MESH
        )

    pl.semaphore_wait(
        barrier, jnp.where(first, 0, 1).astype(jnp.int32) + jnp.where(last, 0, 1).astype(jnp.int32)
    )

    def copy(to):
        return pltpu.make_async_remote_copy(
            src_ref=going,
            dst_ref=held,
            send_sem=send_sem,
            recv_sem=recv_sem,
            device_id={axis: to},
            device_id_type=pl.DeviceIdType.MESH,
        )

    @pl.when(first)
    def _():
        out_ref[...] = init_ref[...]

    @pl.when(jnp.logical_not(first))
    def _():
        copy(lax.rem(me + 1, count)).wait_recv()
        out_ref[...] = held[...]

    @pl.when(jnp.logical_not(last))
    def _():
        columns = out_ref[...].T
        for b in range(blocks):
            going[b : b + 1, :] = (
                jnp.sum(columns[:, b : b + 1] * map_ref[b], axis=0, keepdims=True) + end_ref[b]
            )
        sending = copy(me + 1)
        sending.start()
        sending.wait_send()


def finish_kernel(per, windows, strip, k_ref, vec_ref, v_ref, z_ref, z0_ref, x_ref, w_ref, s_ref, p_ref, acc):
    step = pl.program_id(0)
    eye = iota((BS, BS), 0) == iota((BS, BS), 1)
    tok, refl = iota((WIN, BS), 0), iota((WIN, BS), 1)
    ti, tj = iota((WIN, WIN), 0), iota((WIN, WIN), 1)
    now = [x_ref[b] for b in range(per)]
    for w in range(windows):
        for b in range(per):
            x = now[b]
            k = k_ref[w * BS : (w + 1) * BS, b * BS : (b + 1) * BS]
            v = v_ref[w * WIN : (w + 1) * WIN, b * BS : (b + 1) * BS]
            cum = vec_ref[b, windows + w : windows + w + 1, :]
            tok_col = jnp.sum(jnp.where(refl == REFL * tok, cum, 0.0), axis=1, keepdims=True)
            tok_row = to_row(tok_col, ti == tj)
            z = to_row(jnp.sum(z_ref[b, w] * x, axis=1, keepdims=True), eye) + z0_ref[b, w : w + 1, :]
            take = jnp.where(
                refl // REFL <= tok, jnp.exp(jnp.minimum(cum - tok_col, 0.0)) * z, 0.0
            )
            give = jnp.where(tj <= ti, jnp.exp(jnp.minimum(tok_row - tok_col, 0.0)), 0.0)
            th, tl = split(take)
            gh, gl = split(give)
            rows = (
                jnp.exp(-tok_col) * x
                + (dot(gh, v) + dot(gl, v))
                - (dot(th, k) + dot(tl, k))
            )
            s_ref[w * WIN : (w + 1) * WIN, b * BS : (b + 1) * BS] = rows.astype(BF16)
            now[b] = rows[WIN - 1 : WIN, :]
    half = w_ref.shape[2]
    rows = s_ref[...]
    for side in range(2):
        part = dot(rows, w_ref[side])

        @pl.when(step == 0)
        def _():
            acc[side] = part

        @pl.when(step > 0)
        def _():
            acc[side] += part

    @pl.when(step == pl.num_programs(0) - 1)
    def _():
        for at in range(half // strip):
            for side in range(2):
                p_ref[:, (2 * at + side) * strip : (2 * at + side + 1) * strip] = acc[
                    side, :, at * strip : (at + 1) * strip
                ].astype(BF16)


def shards(key_vectors, beta_values, gate_decay, input_rows, init_state, w_out):
    tok_rows, _, width = key_vectors.shape
    blocks = width // BS
    windows = tok_rows // WIN
    refl_rows = REFL * tok_rows
    per = 2
    keys = key_vectors.reshape(refl_rows, width)
    pos = jnp.arange(WIN)
    up_to = (pos[None, :] <= pos[:, None]).astype(F32)
    cum = jnp.einsum(
        "ts,csb->bct", up_to, gate_decay.reshape(windows, WIN, blocks), precision=lax.Precision.HIGHEST
    )
    vec = jnp.concatenate(
        [
            beta_values.reshape(windows, BS, blocks).transpose(2, 0, 1),
            jnp.repeat(cum, REFL, axis=2),
        ],
        axis=1,
    )
    count = lax.axis_size("tok")
    same_core = [list(range(core, count, 2)) for core in range(2)]
    same_chip = [[2 * chip, 2 * chip + 1] for chip in range(count // 2)]
    half_w = lax.all_gather(w_out, "tok", axis=1, tiled=True, axis_index_groups=same_core)
    full_w = lax.all_gather(half_w, "tok", axis=0, axis_index_groups=same_chip)
    vmem = 48 * 1024 * 1024
    key_spec = pl.BlockSpec((refl_rows, per * BS), lambda g: (0, g))
    vec_spec = pl.BlockSpec((per, 2 * windows, BS), lambda g: (g, 0, 0))
    row_spec = pl.BlockSpec((tok_rows, per * BS), lambda g: (0, g))
    z_spec = pl.BlockSpec((per, windows, BS, BS), lambda g: (g, 0, 0, 0))
    z0_spec = pl.BlockSpec((per, windows, BS), lambda g: (g, 0, 0))
    vector_spec = pl.BlockSpec((per, 1, BS), lambda g: (g, 0, 0))
    maps, ends, z, z0 = pl.pallas_call(
        functools.partial(local_kernel, per, windows),
        grid=(blocks // per,),
        in_specs=[key_spec, vec_spec, row_spec],
        out_specs=[pl.BlockSpec((per, BS, BS), lambda g: (g, 0, 0)), vector_spec, z_spec, z0_spec],
        out_shape=[
            jax.ShapeDtypeStruct((blocks, BS, BS), F32),
            jax.ShapeDtypeStruct((blocks, 1, BS), F32),
            jax.ShapeDtypeStruct((blocks, windows, BS, BS), F32),
            jax.ShapeDtypeStruct((blocks, windows, BS), F32),
        ],
        compiler_params=pltpu.CompilerParams(vmem_limit_bytes=vmem),
        cost_estimate=pl.CostEstimate(
            flops=blocks * windows * 45 * 2 * BS**3, bytes_accessed=10 << 20, transcendentals=0
        ),
        name="local",
    )(keys, vec, input_rows)
    whole = pl.BlockSpec(memory_space=pltpu.VMEM)
    entry = pl.pallas_call(
        functools.partial(chain_kernel, "tok"),
        in_specs=[whole] * 3,
        out_specs=whole,
        out_shape=jax.ShapeDtypeStruct((blocks, BS), F32),
        scratch_shapes=[
            pltpu.VMEM((blocks, BS), F32),
            pltpu.VMEM((blocks, BS), F32),
            pltpu.SemaphoreType.DMA,
            pltpu.SemaphoreType.DMA,
        ],
        compiler_params=pltpu.CompilerParams(
            collective_id=0, has_side_effects=True, vmem_limit_bytes=vmem
        ),
        cost_estimate=pl.CostEstimate(flops=60_000_000, bytes_accessed=60 << 20, transcendentals=0),
        name="chain",
    )(maps, ends, init_state.reshape(blocks, BS))
    out = w_out.shape[1] * lax.axis_size("tok")
    strip = w_out.shape[1] if w_out.shape[1] % BS == 0 else out // 2
    states, projected = pl.pallas_call(
        functools.partial(finish_kernel, per, windows, strip),
        grid=(blocks // per,),
        in_specs=[
            key_spec,
            vec_spec,
            row_spec,
            z_spec,
            z0_spec,
            vector_spec,
            pl.BlockSpec((2, per * BS, out // 2), lambda g: (0, g, 0)),
        ],
        out_specs=[row_spec, pl.BlockSpec((tok_rows, out), lambda g: (0, 0))],
        out_shape=[
            jax.ShapeDtypeStruct((tok_rows, width), BF16),
            jax.ShapeDtypeStruct((tok_rows, out), BF16),
        ],
        scratch_shapes=[pltpu.VMEM((2, tok_rows, out // 2), F32)],
        compiler_params=pltpu.CompilerParams(vmem_limit_bytes=vmem),
        name="finish",
    )(keys, vec, input_rows, z, z0, entry.reshape(blocks, 1, BS), full_w)
    if strip != w_out.shape[1]:
        projected = (
            projected.reshape(tok_rows, 2, count // 2, w_out.shape[1])
            .transpose(0, 2, 1, 3)
            .reshape(tok_rows, out)
        )
    return (states, projected)


def solution(mesh):
    return jax.shard_map(
        shards,
        mesh=mesh,
        in_specs=(
            P(("groups", "tok"), None, None),
            P(("groups", "tok"), None, None),
            P(("groups", "tok"), None),
            P(("groups", "tok"), None),
            P("groups"),
            P(None, "tok"),
        ),
        out_specs=(P(("groups", "tok"), None), P(("groups", "tok"), None)),
        check_vma=False,
    )
```

```python
import functools
import jax
import jax.numpy as jnp
from jax import lax
from jax.experimental import pallas as pl
from jax.experimental.pallas import tpu as pltpu
from jax.sharding import PartitionSpec as P

BS = 128
REFL = 4
WIN = BS // REFL
epsilon = 1e-06
F32 = jnp.float32
BF16 = jnp.bfloat16


def iota(shape, dim):
    return lax.broadcasted_iota(jnp.int32, shape, dim)


def split(a):
    high = a.astype(BF16)
    return high, (a - high.astype(F32)).astype(BF16)


def dot(a, b, dims=((1,), (0,))):
    return lax.dot_general(a, b, (dims, ((), ())), preferred_element_type=F32)


def dot3(a, b):
    (ah, al), (bh, bl) = a, b
    return dot(ah, bh) + (dot(al, bh) + dot(ah, bl))


def to_col(row, eye):
    return jnp.sum(jnp.where(eye, row, 0.0), axis=1, keepdims=True)


def to_row(col, eye):
    return jnp.sum(jnp.where(eye, col, 0.0), axis=0, keepdims=True)


def local_kernel(per, windows, k_ref, vec_ref, v_ref, map_ref, end_ref, z_ref, z0_ref):
    i, j = iota((BS, BS), 0), iota((BS, BS), 1)
    eye = i == j
    eye_f = eye.astype(F32)
    tok, refl = iota((WIN, BS), 0), iota((WIN, BS), 1)
    systems = [(b, w) for b in range(per) for w in range(windows)]

    keys = {}
    a_mats, col_q, push, cums = {}, {}, {}, {}
    for b, w in systems:
        k = k_ref[w * BS : (w + 1) * BS, b * BS : (b + 1) * BS]
        v = v_ref[w * WIN : (w + 1) * WIN, b * BS : (b + 1) * BS]
        beta = vec_ref[b, w : w + 1, :]
        cum = vec_ref[b, windows + w : windows + w + 1, :]
        cum_col = to_col(cum, eye)
        tok_col = jnp.sum(jnp.where(refl == REFL * tok, cum, 0.0), axis=1, keepdims=True)
        gram = dot(k, k, ((1,), (1,)))
        q_row = beta / (to_row(gram, eye) + epsilon)
        q_col = to_col(q_row, eye)
        a_mats[b, w] = jnp.where(
            j < i, q_col * jnp.exp(jnp.minimum(cum - cum_col, 0.0)) * gram, 0.0
        )
        feed = dot(v, k, ((1,), (1,)))
        weigh = jnp.where(
            tok < refl // REFL, jnp.exp(jnp.minimum(tok_col - cum, 0.0)) * feed, 0.0
        )
        push[b, w] = q_row * jnp.sum(weigh, axis=0, keepdims=True)
        keys[b, w] = k
        col_q[b, w] = q_row * jnp.exp(-cum)
        cums[b, w] = (cum, cum_col, tok_col)

    inv = {s: jnp.where(eye, 1.0, jnp.where((i // 2 == j // 2), -a_mats[s], 0.0)) for s in systems}
    size = 2
    while size < BS:
        below = (i // (2 * size) == j // (2 * size)) & (i // size != j // size)
        for s in systems:
            t = split(inv[s])
            x = dot3(split(jnp.where(below, a_mats[s], 0.0)), t)
            inv[s] = inv[s] - dot3(t, split(x))
        size *= 2

    maps, ends = {}, {}
    for b, w in systems:
        s = (b, w)
        k = keys[s]
        cum, cum_col, tok_col = cums[s]
        cum_end = cum[:, BS - 1 : BS]
        th, tl = split(inv[s] * col_q[s])
        z = (dot(th, k) + dot(tl, k))
        z0 = jnp.sum(inv[s] * push[s], axis=1, keepdims=True)
        z_ref[b, w] = z
        z0_ref[b, w : w + 1, :] = to_row(z0, eye)
        to_end = jnp.exp(cum_col - cum_end)
        eh, el = split(to_end * z)
        maps[s] = jnp.exp(-cum_end) * eye_f - (
            dot(eh, k, ((0,), (0,))) + dot(el, k, ((0,), (0,)))
        )
        v = v_ref[w * WIN : (w + 1) * WIN, b * BS : (b + 1) * BS].astype(F32)
        ends[s] = jnp.sum(jnp.exp(tok_col - cum_end) * v, axis=0, keepdims=True) - jnp.sum(
            (to_end * z0) * k.astype(F32), axis=0, keepdims=True
        )

    for b in range(per):
        end = ends[b, 0]
        total = maps[b, 0]
        for w in range(1, windows):
            end = jnp.sum(to_col(end, eye) * maps[b, w], axis=0, keepdims=True) + ends[b, w]
            total = dot3(split(total), split(maps[b, w]))
        map_ref[b] = total
        end_ref[b] = end


def chain_kernel(axis, map_ref, end_ref, init_ref, out_ref, held, going, send_sem, recv_sem):
    blocks = init_ref.shape[0]
    count, me = lax.axis_size(axis), lax.axis_index(axis)
    first, last = me == 0, me == count - 1
    barrier = pltpu.get_barrier_semaphore()

    @pl.when(jnp.logical_not(first))
    def _():
        pl.semaphore_signal(
            barrier, inc=1, device_id={axis: me - 1}, device_id_type=pl.DeviceIdType.MESH
        )

    @pl.when(jnp.logical_not(last))
    def _():
        pl.semaphore_signal(
            barrier, inc=1, device_id={axis: me + 1}, device_id_type=pl.DeviceIdType.MESH
        )

    pl.semaphore_wait(
        barrier, jnp.where(first, 0, 1).astype(jnp.int32) + jnp.where(last, 0, 1).astype(jnp.int32)
    )

    def copy(to):
        return pltpu.make_async_remote_copy(
            src_ref=going,
            dst_ref=held,
            send_sem=send_sem,
            recv_sem=recv_sem,
            device_id={axis: to},
            device_id_type=pl.DeviceIdType.MESH,
        )

    @pl.when(first)
    def _():
        out_ref[...] = init_ref[...]

    @pl.when(jnp.logical_not(first))
    def _():
        copy(lax.rem(me + 1, count)).wait_recv()
        out_ref[...] = held[...]

    @pl.when(jnp.logical_not(last))
    def _():
        columns = out_ref[...].T
        for b in range(blocks):
            going[b : b + 1, :] = (
                jnp.sum(columns[:, b : b + 1] * map_ref[b], axis=0, keepdims=True) + end_ref[b]
            )
        sending = copy(me + 1)
        sending.start()
        sending.wait_send()


def states_kernel(per, windows, k_ref, vec_ref, v_ref, z_ref, z0_ref, x_ref, s_ref):
    eye = iota((BS, BS), 0) == iota((BS, BS), 1)
    tok, refl = iota((WIN, BS), 0), iota((WIN, BS), 1)
    ti, tj = iota((WIN, WIN), 0), iota((WIN, WIN), 1)
    now = [x_ref[b] for b in range(per)]
    for w in range(windows):
        for b in range(per):
            x = now[b]
            k = k_ref[w * BS : (w + 1) * BS, b * BS : (b + 1) * BS]
            v = v_ref[w * WIN : (w + 1) * WIN, b * BS : (b + 1) * BS]
            cum = vec_ref[b, windows + w : windows + w + 1, :]
            tok_col = jnp.sum(jnp.where(refl == REFL * tok, cum, 0.0), axis=1, keepdims=True)
            tok_row = to_row(tok_col, ti == tj)
            z = to_row(jnp.sum(z_ref[b, w] * x, axis=1, keepdims=True), eye) + z0_ref[b, w : w + 1, :]
            take = jnp.where(
                refl // REFL <= tok, jnp.exp(jnp.minimum(cum - tok_col, 0.0)) * z, 0.0
            )
            give = jnp.where(tj <= ti, jnp.exp(jnp.minimum(tok_row - tok_col, 0.0)), 0.0)
            th, tl = split(take)
            gh, gl = split(give)
            rows = (
                jnp.exp(-tok_col) * x
                + (dot(gh, v) + dot(gl, v))
                - (dot(th, k) + dot(tl, k))
            )
            s_ref[w * WIN : (w + 1) * WIN, b * BS : (b + 1) * BS] = rows.astype(BF16)
            now[b] = rows[WIN - 1 : WIN, :]


def shards(key_vectors, beta_values, gate_decay, input_rows, init_state, w_out):
    tok_rows, _, width = key_vectors.shape
    blocks = width // BS
    windows = tok_rows // WIN
    refl_rows = REFL * tok_rows
    per = 2
    keys = key_vectors.reshape(refl_rows, width)
    pos = jnp.arange(WIN)
    up_to = (pos[None, :] <= pos[:, None]).astype(F32)
    cum = jnp.einsum(
        "ts,csb->bct", up_to, gate_decay.reshape(windows, WIN, blocks), precision=lax.Precision.HIGHEST
    )
    vec = jnp.concatenate(
        [
            beta_values.reshape(windows, BS, blocks).transpose(2, 0, 1),
            jnp.repeat(cum, REFL, axis=2),
        ],
        axis=1,
    )
    full_w = lax.all_gather(w_out, "tok", axis=1, tiled=True)
    vmem = 48 * 1024 * 1024
    key_spec = pl.BlockSpec((refl_rows, per * BS), lambda g: (0, g))
    vec_spec = pl.BlockSpec((per, 2 * windows, BS), lambda g: (g, 0, 0))
    row_spec = pl.BlockSpec((tok_rows, per * BS), lambda g: (0, g))
    z_spec = pl.BlockSpec((per, windows, BS, BS), lambda g: (g, 0, 0, 0))
    z0_spec = pl.BlockSpec((per, windows, BS), lambda g: (g, 0, 0))
    vector_spec = pl.BlockSpec((per, 1, BS), lambda g: (g, 0, 0))
    maps, ends, z, z0 = pl.pallas_call(
        functools.partial(local_kernel, per, windows),
        grid=(blocks // per,),
        in_specs=[key_spec, vec_spec, row_spec],
        out_specs=[pl.BlockSpec((per, BS, BS), lambda g: (g, 0, 0)), vector_spec, z_spec, z0_spec],
        out_shape=[
            jax.ShapeDtypeStruct((blocks, BS, BS), F32),
            jax.ShapeDtypeStruct((blocks, 1, BS), F32),
            jax.ShapeDtypeStruct((blocks, windows, BS, BS), F32),
            jax.ShapeDtypeStruct((blocks, windows, BS), F32),
        ],
        compiler_params=pltpu.CompilerParams(vmem_limit_bytes=vmem),
        cost_estimate=pl.CostEstimate(
            flops=blocks * windows * 45 * 2 * BS**3, bytes_accessed=10 << 20, transcendentals=0
        ),
        name="local",
    )(keys, vec, input_rows)
    whole = pl.BlockSpec(memory_space=pltpu.VMEM)
    entry = pl.pallas_call(
        functools.partial(chain_kernel, "tok"),
        in_specs=[whole] * 3,
        out_specs=whole,
        out_shape=jax.ShapeDtypeStruct((blocks, BS), F32),
        scratch_shapes=[
            pltpu.VMEM((blocks, BS), F32),
            pltpu.VMEM((blocks, BS), F32),
            pltpu.SemaphoreType.DMA,
            pltpu.SemaphoreType.DMA,
        ],
        compiler_params=pltpu.CompilerParams(
            collective_id=0, has_side_effects=True, vmem_limit_bytes=vmem
        ),
        cost_estimate=pl.CostEstimate(flops=60_000_000, bytes_accessed=60 << 20, transcendentals=0),
        name="chain",
    )(maps, ends, init_state.reshape(blocks, BS))
    more = 4
    states = pl.pallas_call(
        functools.partial(states_kernel, more, windows),
        grid=(blocks // more,),
        in_specs=[
            pl.BlockSpec((refl_rows, more * BS), lambda g: (0, g)),
            pl.BlockSpec((more, 2 * windows, BS), lambda g: (g, 0, 0)),
            pl.BlockSpec((tok_rows, more * BS), lambda g: (0, g)),
            pl.BlockSpec((more, windows, BS, BS), lambda g: (g, 0, 0, 0)),
            pl.BlockSpec((more, windows, BS), lambda g: (g, 0, 0)),
            pl.BlockSpec((more, 1, BS), lambda g: (g, 0, 0)),
        ],
        out_specs=pl.BlockSpec((tok_rows, more * BS), lambda g: (0, g)),
        out_shape=jax.ShapeDtypeStruct((tok_rows, width), BF16),
        compiler_params=pltpu.CompilerParams(vmem_limit_bytes=vmem),
        cost_estimate=pl.CostEstimate(
            flops=blocks * windows * 8 * BS**3, bytes_accessed=10 << 20, transcendentals=0
        ),
        name="states",
    )(keys, vec, input_rows, z, z0, entry.reshape(blocks, 1, BS))
    projected = jnp.dot(states, full_w, preferred_element_type=F32).astype(BF16)
    return (states, projected)


def solution(mesh):
    return jax.shard_map(
        shards,
        mesh=mesh,
        in_specs=(
            P(("groups", "tok"), None, None),
            P(("groups", "tok"), None, None),
            P(("groups", "tok"), None),
            P(("groups", "tok"), None),
            P("groups"),
            P(None, "tok"),
        ),
        out_specs=(P(("groups", "tok"), None), P(("groups", "tok"), None)),
        check_vma=False,
    )
```

```python
import functools
import jax
import jax.numpy as jnp
from jax import lax
from jax.experimental import pallas as pl
from jax.experimental.pallas import tpu as pltpu
from jax.sharding import PartitionSpec as P

BS = 128
REFL = 4
WIN = BS // REFL
epsilon = 1e-06
F32 = jnp.float32
BF16 = jnp.bfloat16


def iota(shape, dim):
    return lax.broadcasted_iota(jnp.int32, shape, dim)


def split(a):
    high = a.astype(BF16)
    return high, (a - high.astype(F32)).astype(BF16)


def dot(a, b, dims=((1,), (0,))):
    return lax.dot_general(a, b, (dims, ((), ())), preferred_element_type=F32)


def dot3(a, b):
    (ah, al), (bh, bl) = a, b
    return dot(ah, bh) + (dot(al, bh) + dot(ah, bl))


def to_col(row, eye):
    return jnp.sum(jnp.where(eye, row, 0.0), axis=1, keepdims=True)


def to_row(col, eye):
    return jnp.sum(jnp.where(eye, col, 0.0), axis=0, keepdims=True)


def local_kernel(per, windows, k_ref, vec_ref, v_ref, pack_ref, z_ref, z0_ref):
    i, j = iota((BS, BS), 0), iota((BS, BS), 1)
    eye = i == j
    eye_f = eye.astype(F32)
    tok, refl = iota((WIN, BS), 0), iota((WIN, BS), 1)
    systems = [(b, w) for b in range(per) for w in range(windows)]

    keys = {}
    a_mats, col_q, push, cums = {}, {}, {}, {}
    for b, w in systems:
        k = k_ref[w * BS : (w + 1) * BS, b * BS : (b + 1) * BS]
        v = v_ref[w * WIN : (w + 1) * WIN, b * BS : (b + 1) * BS]
        beta = vec_ref[b, w : w + 1, :]
        cum = vec_ref[b, windows + w : windows + w + 1, :]
        cum_col = to_col(cum, eye)
        tok_col = jnp.sum(jnp.where(refl == REFL * tok, cum, 0.0), axis=1, keepdims=True)
        gram = dot(k, k, ((1,), (1,)))
        q_row = beta / (to_row(gram, eye) + epsilon)
        q_col = to_col(q_row, eye)
        a_mats[b, w] = jnp.where(
            j < i, q_col * jnp.exp(jnp.minimum(cum - cum_col, 0.0)) * gram, 0.0
        )
        feed = dot(v, k, ((1,), (1,)))
        weigh = jnp.where(
            tok < refl // REFL, jnp.exp(jnp.minimum(tok_col - cum, 0.0)) * feed, 0.0
        )
        push[b, w] = q_row * jnp.sum(weigh, axis=0, keepdims=True)
        keys[b, w] = k
        col_q[b, w] = q_row * jnp.exp(-cum)
        cums[b, w] = (cum, cum_col, tok_col)

    inv = {s: jnp.where(eye, 1.0, jnp.where((i // 2 == j // 2), -a_mats[s], 0.0)) for s in systems}
    size = 2
    while size < BS:
        below = (i // (2 * size) == j // (2 * size)) & (i // size != j // size)
        for s in systems:
            t = split(inv[s])
            x = dot3(split(jnp.where(below, a_mats[s], 0.0)), t)
            inv[s] = inv[s] - dot3(t, split(x))
        size *= 2

    maps, ends = {}, {}
    for b, w in systems:
        s = (b, w)
        k = keys[s]
        cum, cum_col, tok_col = cums[s]
        cum_end = cum[:, BS - 1 : BS]
        th, tl = split(inv[s] * col_q[s])
        z = (dot(th, k) + dot(tl, k))
        z0 = jnp.sum(inv[s] * push[s], axis=1, keepdims=True)
        z_ref[b, w] = z
        z0_ref[b, w : w + 1, :] = to_row(z0, eye)
        to_end = jnp.exp(cum_col - cum_end)
        eh, el = split(to_end * z)
        maps[s] = jnp.exp(-cum_end) * eye_f - (
            dot(eh, k, ((0,), (0,))) + dot(el, k, ((0,), (0,)))
        )
        v = v_ref[w * WIN : (w + 1) * WIN, b * BS : (b + 1) * BS].astype(F32)
        ends[s] = jnp.sum(jnp.exp(tok_col - cum_end) * v, axis=0, keepdims=True) - jnp.sum(
            (to_end * z0) * k.astype(F32), axis=0, keepdims=True
        )

    for b in range(per):
        end = ends[b, 0]
        total = maps[b, 0]
        for w in range(1, windows):
            end = jnp.sum(to_col(end, eye) * maps[b, w], axis=0, keepdims=True) + ends[b, w]
            total = dot3(split(total), split(maps[b, w]))
        pack_ref[b, :BS, :] = total
        pack_ref[b, BS:, :] = jnp.broadcast_to(end, (8, BS))


def chain_kernel(axis, own_ref, sib_ref, init_ref, out_ref, held, going, pair, send_sem, recv_sem):
    blocks = init_ref.shape[0]
    count, me = lax.axis_size(axis), lax.axis_index(axis)
    first, last = me < 2, me >= count - 2
    odd = lax.rem(me, 2) == 1
    barrier = pltpu.get_barrier_semaphore()

    @pl.when(jnp.logical_not(first))
    def _():
        pl.semaphore_signal(
            barrier, inc=1, device_id={axis: me - 2}, device_id_type=pl.DeviceIdType.MESH
        )

    @pl.when(jnp.logical_not(last))
    def _():
        pl.semaphore_signal(
            barrier, inc=1, device_id={axis: me + 2}, device_id_type=pl.DeviceIdType.MESH
        )

    for b in range(blocks):
        early = jnp.where(odd, sib_ref[b], own_ref[b])
        late = jnp.where(odd, own_ref[b], sib_ref[b])
        eye = iota((BS, BS), 0) == iota((BS, BS), 1)
        pair[b, :BS, :] = dot3(split(early[:BS]), split(late[:BS]))
        carried = jnp.sum(to_col(early[BS : BS + 1], eye) * late[:BS], axis=0, keepdims=True)
        pair[b, BS:, :] = jnp.broadcast_to(carried + late[BS : BS + 1], (8, BS))

    pl.semaphore_wait(
        barrier, jnp.where(first, 0, 1).astype(jnp.int32) + jnp.where(last, 0, 1).astype(jnp.int32)
    )

    def copy(to):
        return pltpu.make_async_remote_copy(
            src_ref=going,
            dst_ref=held,
            send_sem=send_sem,
            recv_sem=recv_sem,
            device_id={axis: to},
            device_id_type=pl.DeviceIdType.MESH,
        )

    def push(source, target):
        columns = out_ref[...].T
        for b in range(blocks):
            target[b : b + 1, :] = (
                jnp.sum(columns[:, b : b + 1] * source[b, :BS, :], axis=0, keepdims=True)
                + source[b, BS : BS + 1, :]
            )

    @pl.when(first)
    def _():
        out_ref[...] = init_ref[...]

    @pl.when(jnp.logical_not(first))
    def _():
        copy(lax.rem(me + 2, count)).wait_recv()
        out_ref[...] = held[...]

    @pl.when(jnp.logical_not(last))
    def _():
        push(pair, going)
        copy(me + 2).start()

    @pl.when(odd)
    def _():
        push(sib_ref, out_ref)

    @pl.when(jnp.logical_not(last))
    def _():
        copy(me + 2).wait_send()


def states_kernel(per, windows, k_ref, vec_ref, v_ref, z_ref, z0_ref, x_ref, s_ref):
    eye = iota((BS, BS), 0) == iota((BS, BS), 1)
    tok, refl = iota((WIN, BS), 0), iota((WIN, BS), 1)
    ti, tj = iota((WIN, WIN), 0), iota((WIN, WIN), 1)
    now = [x_ref[b] for b in range(per)]
    for w in range(windows):
        for b in range(per):
            x = now[b]
            k = k_ref[w * BS : (w + 1) * BS, b * BS : (b + 1) * BS]
            v = v_ref[w * WIN : (w + 1) * WIN, b * BS : (b + 1) * BS]
            cum = vec_ref[b, windows + w : windows + w + 1, :]
            tok_col = jnp.sum(jnp.where(refl == REFL * tok, cum, 0.0), axis=1, keepdims=True)
            tok_row = to_row(tok_col, ti == tj)
            z = to_row(jnp.sum(z_ref[b, w] * x, axis=1, keepdims=True), eye) + z0_ref[b, w : w + 1, :]
            take = jnp.where(
                refl // REFL <= tok, jnp.exp(jnp.minimum(cum - tok_col, 0.0)) * z, 0.0
            )
            give = jnp.where(tj <= ti, jnp.exp(jnp.minimum(tok_row - tok_col, 0.0)), 0.0)
            th, tl = split(take)
            gh, gl = split(give)
            rows = (
                jnp.exp(-tok_col) * x
                + (dot(gh, v) + dot(gl, v))
                - (dot(th, k) + dot(tl, k))
            )
            s_ref[w * WIN : (w + 1) * WIN, b * BS : (b + 1) * BS] = rows.astype(BF16)
            now[b] = rows[WIN - 1 : WIN, :]


def shards(key_vectors, beta_values, gate_decay, input_rows, init_state, w_out):
    tok_rows, _, width = key_vectors.shape
    blocks = width // BS
    windows = tok_rows // WIN
    refl_rows = REFL * tok_rows
    per = 2
    keys = key_vectors.reshape(refl_rows, width)
    pos = jnp.arange(WIN)
    up_to = (pos[None, :] <= pos[:, None]).astype(F32)
    cum = jnp.einsum(
        "ts,csb->bct", up_to, gate_decay.reshape(windows, WIN, blocks), precision=lax.Precision.HIGHEST
    )
    vec = jnp.concatenate(
        [
            beta_values.reshape(windows, BS, blocks).transpose(2, 0, 1),
            jnp.repeat(cum, REFL, axis=2),
        ],
        axis=1,
    )
    count = lax.axis_size("tok")
    if count == 16:
        order = [0, 1, 4, 5, 8, 9, 12, 13, 15, 14, 11, 10, 7, 6, 3, 2]
    else:
        order = list(range(0, count, 2)) + list(range(1, count, 2))[::-1]
    full_w = lax.all_gather(w_out, "tok", axis=1, tiled=True, axis_index_groups=[order])
    vmem = 48 * 1024 * 1024
    key_spec = pl.BlockSpec((refl_rows, per * BS), lambda g: (0, g))
    vec_spec = pl.BlockSpec((per, 2 * windows, BS), lambda g: (g, 0, 0))
    row_spec = pl.BlockSpec((tok_rows, per * BS), lambda g: (0, g))
    z_spec = pl.BlockSpec((per, windows, BS, BS), lambda g: (g, 0, 0, 0))
    z0_spec = pl.BlockSpec((per, windows, BS), lambda g: (g, 0, 0))
    pack, z, z0 = pl.pallas_call(
        functools.partial(local_kernel, per, windows),
        grid=(blocks // per,),
        in_specs=[key_spec, vec_spec, row_spec],
        out_specs=[pl.BlockSpec((per, BS + 8, BS), lambda g: (g, 0, 0)), z_spec, z0_spec],
        out_shape=[
            jax.ShapeDtypeStruct((blocks, BS + 8, BS), F32),
            jax.ShapeDtypeStruct((blocks, windows, BS, BS), F32),
            jax.ShapeDtypeStruct((blocks, windows, BS), F32),
        ],
        compiler_params=pltpu.CompilerParams(vmem_limit_bytes=vmem),
        cost_estimate=pl.CostEstimate(
            flops=blocks * windows * 45 * 2 * BS**3, bytes_accessed=10 << 20, transcendentals=0
        ),
        name="local",
    )(keys, vec, input_rows)
    whole = pl.BlockSpec(memory_space=pltpu.VMEM)
    sibling = lax.ppermute(pack, "tok", [(at, at ^ 1) for at in range(count)])
    entry = pl.pallas_call(
        functools.partial(chain_kernel, "tok"),
        in_specs=[whole] * 3,
        out_specs=whole,
        out_shape=jax.ShapeDtypeStruct((blocks, BS), F32),
        scratch_shapes=[
            pltpu.VMEM((blocks, BS), F32),
            pltpu.VMEM((blocks, BS), F32),
            pltpu.VMEM((blocks, BS + 8, BS), F32),
            pltpu.SemaphoreType.DMA,
            pltpu.SemaphoreType.DMA,
        ],
        compiler_params=pltpu.CompilerParams(
            collective_id=0, has_side_effects=True, vmem_limit_bytes=vmem
        ),
        cost_estimate=pl.CostEstimate(flops=60_000_000, bytes_accessed=60 << 20, transcendentals=0),
        name="chain",
    )(pack, sibling, init_state.reshape(blocks, BS))
    more = 4
    states = pl.pallas_call(
        functools.partial(states_kernel, more, windows),
        grid=(blocks // more,),
        in_specs=[
            pl.BlockSpec((refl_rows, more * BS), lambda g: (0, g)),
            pl.BlockSpec((more, 2 * windows, BS), lambda g: (g, 0, 0)),
            pl.BlockSpec((tok_rows, more * BS), lambda g: (0, g)),
            pl.BlockSpec((more, windows, BS, BS), lambda g: (g, 0, 0, 0)),
            pl.BlockSpec((more, windows, BS), lambda g: (g, 0, 0)),
            pl.BlockSpec((more, 1, BS), lambda g: (g, 0, 0)),
        ],
        out_specs=pl.BlockSpec((tok_rows, more * BS), lambda g: (0, g)),
        out_shape=jax.ShapeDtypeStruct((tok_rows, width), BF16),
        compiler_params=pltpu.CompilerParams(vmem_limit_bytes=vmem),
        cost_estimate=pl.CostEstimate(
            flops=blocks * windows * 8 * BS**3, bytes_accessed=10 << 20, transcendentals=0
        ),
        name="states",
    )(keys, vec, input_rows, z, z0, entry.reshape(blocks, 1, BS))
    projected = jnp.dot(states, full_w, preferred_element_type=F32).astype(BF16)
    wide = w_out.shape[1]
    projected = jnp.concatenate(
        [
            projected[:, order.index(at) * wide : (order.index(at) + 1) * wide]
            for at in range(count)
        ],
        axis=1,
    )
    return (states, projected)


def solution(mesh):
    return jax.shard_map(
        shards,
        mesh=mesh,
        in_specs=(
            P(("groups", "tok"), None, None),
            P(("groups", "tok"), None, None),
            P(("groups", "tok"), None),
            P(("groups", "tok"), None),
            P("groups"),
            P(None, "tok"),
        ),
        out_specs=(P(("groups", "tok"), None), P(("groups", "tok"), None)),
        check_vma=False,
    )
```

```python
import functools
import jax
import jax.numpy as jnp
from jax import lax
from jax.experimental import pallas as pl
from jax.experimental.pallas import tpu as pltpu
from jax.sharding import PartitionSpec as P

BS = 128
REFL = 4
WIN = BS // REFL
epsilon = 1e-06
F32 = jnp.float32
BF16 = jnp.bfloat16


def iota(shape, dim):
    return lax.broadcasted_iota(jnp.int32, shape, dim)


def split(a):
    high = a.astype(BF16)
    return high, (a - high.astype(F32)).astype(BF16)


def dot(a, b, dims=((1,), (0,))):
    return lax.dot_general(a, b, (dims, ((), ())), preferred_element_type=F32)


def dot3(a, b):
    (ah, al), (bh, bl) = a, b
    return dot(ah, bh) + (dot(al, bh) + dot(ah, bl))


def to_col(row, eye):
    return jnp.sum(jnp.where(eye, row, 0.0), axis=1, keepdims=True)


def to_row(col, eye):
    return jnp.sum(jnp.where(eye, col, 0.0), axis=0, keepdims=True)


def local_kernel(per, windows, k_ref, vec_ref, v_ref, pack_ref, z_ref, z0_ref):
    i, j = iota((BS, BS), 0), iota((BS, BS), 1)
    eye = i == j
    eye_f = eye.astype(F32)
    tok, refl = iota((WIN, BS), 0), iota((WIN, BS), 1)
    systems = [(b, w) for b in range(per) for w in range(windows)]

    keys = {}
    a_mats, col_q, push, cums = {}, {}, {}, {}
    for b, w in systems:
        k = k_ref[w * BS : (w + 1) * BS, b * BS : (b + 1) * BS]
        v = v_ref[w * WIN : (w + 1) * WIN, b * BS : (b + 1) * BS]
        beta = vec_ref[b, w : w + 1, :]
        cum = vec_ref[b, windows + w : windows + w + 1, :]
        cum_col = to_col(cum, eye)
        tok_col = jnp.sum(jnp.where(refl == REFL * tok, cum, 0.0), axis=1, keepdims=True)
        gram = dot(k, k, ((1,), (1,)))
        q_row = beta / (to_row(gram, eye) + epsilon)
        q_col = to_col(q_row, eye)
        a_mats[b, w] = jnp.where(
            j < i, q_col * jnp.exp(jnp.minimum(cum - cum_col, 0.0)) * gram, 0.0
        )
        feed = dot(v, k, ((1,), (1,)))
        weigh = jnp.where(
            tok < refl // REFL, jnp.exp(jnp.minimum(tok_col - cum, 0.0)) * feed, 0.0
        )
        push[b, w] = q_row * jnp.sum(weigh, axis=0, keepdims=True)
        keys[b, w] = k
        col_q[b, w] = q_row * jnp.exp(-cum)
        cums[b, w] = (cum, cum_col, tok_col)

    inv = {s: jnp.where(eye, 1.0, jnp.where((i // 2 == j // 2), -a_mats[s], 0.0)) for s in systems}
    size = 2
    while size < BS:
        below = (i // (2 * size) == j // (2 * size)) & (i // size != j // size)
        for s in systems:
            t = split(inv[s])
            x = dot3(split(jnp.where(below, a_mats[s], 0.0)), t)
            inv[s] = inv[s] - dot3(t, split(x))
        size *= 2

    maps, ends = {}, {}
    for b, w in systems:
        s = (b, w)
        k = keys[s]
        cum, cum_col, tok_col = cums[s]
        cum_end = cum[:, BS - 1 : BS]
        th, tl = split(inv[s] * col_q[s])
        z = (dot(th, k) + dot(tl, k))
        z0 = jnp.sum(inv[s] * push[s], axis=1, keepdims=True)
        z_ref[b, w] = z
        z0_ref[b, w : w + 1, :] = to_row(z0, eye)
        to_end = jnp.exp(cum_col - cum_end)
        eh, el = split(to_end * z)
        maps[s] = jnp.exp(-cum_end) * eye_f - (
            dot(eh, k, ((0,), (0,))) + dot(el, k, ((0,), (0,)))
        )
        v = v_ref[w * WIN : (w + 1) * WIN, b * BS : (b + 1) * BS].astype(F32)
        ends[s] = jnp.sum(jnp.exp(tok_col - cum_end) * v, axis=0, keepdims=True) - jnp.sum(
            (to_end * z0) * k.astype(F32), axis=0, keepdims=True
        )

    for b in range(per):
        end = ends[b, 0]
        total = maps[b, 0]
        for w in range(1, windows):
            end = jnp.sum(to_col(end, eye) * maps[b, w], axis=0, keepdims=True) + ends[b, w]
            total = dot3(split(total), split(maps[b, w]))
        pack_ref[b, :BS, :] = total
        pack_ref[b, BS:, :] = jnp.broadcast_to(end, (8, BS))


def chain_kernel(axis, own_ref, sib_ref, init_ref, out_ref, held, going, pair, send_sem, recv_sem):
    blocks = init_ref.shape[0]
    count, me = lax.axis_size(axis), lax.axis_index(axis)
    first, last = me < 2, me >= count - 2
    odd = lax.rem(me, 2) == 1
    barrier = pltpu.get_barrier_semaphore()

    @pl.when(jnp.logical_not(first))
    def _():
        pl.semaphore_signal(
            barrier, inc=1, device_id={axis: me - 2}, device_id_type=pl.DeviceIdType.MESH
        )

    @pl.when(jnp.logical_not(last))
    def _():
        pl.semaphore_signal(
            barrier, inc=1, device_id={axis: me + 2}, device_id_type=pl.DeviceIdType.MESH
        )

    for b in range(blocks):
        early = jnp.where(odd, sib_ref[b], own_ref[b])
        late = jnp.where(odd, own_ref[b], sib_ref[b])
        eye = iota((BS, BS), 0) == iota((BS, BS), 1)
        pair[b, :BS, :] = dot3(split(early[:BS]), split(late[:BS]))
        carried = jnp.sum(to_col(early[BS : BS + 1], eye) * late[:BS], axis=0, keepdims=True)
        pair[b, BS:, :] = jnp.broadcast_to(carried + late[BS : BS + 1], (8, BS))

    pl.semaphore_wait(
        barrier, jnp.where(first, 0, 1).astype(jnp.int32) + jnp.where(last, 0, 1).astype(jnp.int32)
    )

    def copy(to):
        return pltpu.make_async_remote_copy(
            src_ref=going,
            dst_ref=held,
            send_sem=send_sem,
            recv_sem=recv_sem,
            device_id={axis: to},
            device_id_type=pl.DeviceIdType.MESH,
        )

    def push(source, target):
        columns = out_ref[...].T
        for b in range(blocks):
            target[b : b + 1, :] = (
                jnp.sum(columns[:, b : b + 1] * source[b, :BS, :], axis=0, keepdims=True)
                + source[b, BS : BS + 1, :]
            )

    @pl.when(first)
    def _():
        out_ref[...] = init_ref[...]

    @pl.when(jnp.logical_not(first))
    def _():
        copy(lax.rem(me + 2, count)).wait_recv()
        out_ref[...] = held[...]

    @pl.when(jnp.logical_not(last))
    def _():
        push(pair, going)
        copy(me + 2).start()

    @pl.when(odd)
    def _():
        push(sib_ref, out_ref)

    @pl.when(jnp.logical_not(last))
    def _():
        copy(me + 2).wait_send()


def states_kernel(per, windows, k_ref, vec_ref, v_ref, z_ref, z0_ref, x_ref, s_ref):
    eye = iota((BS, BS), 0) == iota((BS, BS), 1)
    tok, refl = iota((WIN, BS), 0), iota((WIN, BS), 1)
    ti, tj = iota((WIN, WIN), 0), iota((WIN, WIN), 1)
    now = [x_ref[b] for b in range(per)]
    for w in range(windows):
        for b in range(per):
            x = now[b]
            k = k_ref[w * BS : (w + 1) * BS, b * BS : (b + 1) * BS]
            v = v_ref[w * WIN : (w + 1) * WIN, b * BS : (b + 1) * BS]
            cum = vec_ref[b, windows + w : windows + w + 1, :]
            tok_col = jnp.sum(jnp.where(refl == REFL * tok, cum, 0.0), axis=1, keepdims=True)
            tok_row = to_row(tok_col, ti == tj)
            z = to_row(jnp.sum(z_ref[b, w] * x, axis=1, keepdims=True), eye) + z0_ref[b, w : w + 1, :]
            take = jnp.where(
                refl // REFL <= tok, jnp.exp(jnp.minimum(cum - tok_col, 0.0)) * z, 0.0
            )
            give = jnp.where(tj <= ti, jnp.exp(jnp.minimum(tok_row - tok_col, 0.0)), 0.0)
            th, tl = split(take)
            gh, gl = split(give)
            rows = (
                jnp.exp(-tok_col) * x
                + (dot(gh, v) + dot(gl, v))
                - (dot(th, k) + dot(tl, k))
            )
            s_ref[w * WIN : (w + 1) * WIN, b * BS : (b + 1) * BS] = rows.astype(BF16)
            now[b] = rows[WIN - 1 : WIN, :]


def shards(key_vectors, beta_values, gate_decay, input_rows, init_state, w_out):
    tok_rows, _, width = key_vectors.shape
    blocks = width // BS
    windows = tok_rows // WIN
    refl_rows = REFL * tok_rows
    per = 4
    keys = key_vectors.reshape(refl_rows, width)
    pos = jnp.arange(WIN)
    up_to = (pos[None, :] <= pos[:, None]).astype(F32)
    cum = jnp.einsum(
        "ts,csb->bct", up_to, gate_decay.reshape(windows, WIN, blocks), precision=lax.Precision.HIGHEST
    )
    vec = jnp.concatenate(
        [
            beta_values.reshape(windows, BS, blocks).transpose(2, 0, 1),
            jnp.repeat(cum, REFL, axis=2),
        ],
        axis=1,
    )
    count = lax.axis_size("tok")
    if count == 16:
        order = [0, 1, 4, 5, 8, 9, 12, 13, 15, 14, 11, 10, 7, 6, 3, 2]
    else:
        order = list(range(0, count, 2)) + list(range(1, count, 2))[::-1]
    full_w = lax.all_gather(w_out, "tok", axis=1, tiled=True, axis_index_groups=[order])
    vmem = 48 * 1024 * 1024
    key_spec = pl.BlockSpec((refl_rows, per * BS), lambda g: (0, g))
    vec_spec = pl.BlockSpec((per, 2 * windows, BS), lambda g: (g, 0, 0))
    row_spec = pl.BlockSpec((tok_rows, per * BS), lambda g: (0, g))
    z_spec = pl.BlockSpec((per, windows, BS, BS), lambda g: (g, 0, 0, 0))
    z0_spec = pl.BlockSpec((per, windows, BS), lambda g: (g, 0, 0))
    pack, z, z0 = pl.pallas_call(
        functools.partial(local_kernel, per, windows),
        grid=(blocks // per,),
        in_specs=[key_spec, vec_spec, row_spec],
        out_specs=[pl.BlockSpec((per, BS + 8, BS), lambda g: (g, 0, 0)), z_spec, z0_spec],
        out_shape=[
            jax.ShapeDtypeStruct((blocks, BS + 8, BS), F32),
            jax.ShapeDtypeStruct((blocks, windows, BS, BS), F32),
            jax.ShapeDtypeStruct((blocks, windows, BS), F32),
        ],
        compiler_params=pltpu.CompilerParams(vmem_limit_bytes=vmem),
        cost_estimate=pl.CostEstimate(
            flops=blocks * windows * 45 * 2 * BS**3, bytes_accessed=10 << 20, transcendentals=0
        ),
        name="local",
    )(keys, vec, input_rows)
    whole = pl.BlockSpec(memory_space=pltpu.VMEM)
    sibling = lax.ppermute(pack, "tok", [(at, at ^ 1) for at in range(count)])
    entry = pl.pallas_call(
        functools.partial(chain_kernel, "tok"),
        in_specs=[whole] * 3,
        out_specs=whole,
        out_shape=jax.ShapeDtypeStruct((blocks, BS), F32),
        scratch_shapes=[
            pltpu.VMEM((blocks, BS), F32),
            pltpu.VMEM((blocks, BS), F32),
            pltpu.VMEM((blocks, BS + 8, BS), F32),
            pltpu.SemaphoreType.DMA,
            pltpu.SemaphoreType.DMA,
        ],
        compiler_params=pltpu.CompilerParams(
            collective_id=0, has_side_effects=True, vmem_limit_bytes=vmem
        ),
        cost_estimate=pl.CostEstimate(flops=60_000_000, bytes_accessed=60 << 20, transcendentals=0),
        name="chain",
    )(pack, sibling, init_state.reshape(blocks, BS))
    more = 4
    states = pl.pallas_call(
        functools.partial(states_kernel, more, windows),
        grid=(blocks // more,),
        in_specs=[
            pl.BlockSpec((refl_rows, more * BS), lambda g: (0, g)),
            pl.BlockSpec((more, 2 * windows, BS), lambda g: (g, 0, 0)),
            pl.BlockSpec((tok_rows, more * BS), lambda g: (0, g)),
            pl.BlockSpec((more, windows, BS, BS), lambda g: (g, 0, 0, 0)),
            pl.BlockSpec((more, windows, BS), lambda g: (g, 0, 0)),
            pl.BlockSpec((more, 1, BS), lambda g: (g, 0, 0)),
        ],
        out_specs=pl.BlockSpec((tok_rows, more * BS), lambda g: (0, g)),
        out_shape=jax.ShapeDtypeStruct((tok_rows, width), BF16),
        compiler_params=pltpu.CompilerParams(vmem_limit_bytes=vmem),
        cost_estimate=pl.CostEstimate(
            flops=blocks * windows * 8 * BS**3, bytes_accessed=10 << 20, transcendentals=0
        ),
        name="states",
    )(keys, vec, input_rows, z, z0, entry.reshape(blocks, 1, BS))
    projected = jnp.dot(states, full_w, preferred_element_type=F32).astype(BF16)
    wide = w_out.shape[1]
    projected = jnp.concatenate(
        [
            projected[:, order.index(at) * wide : (order.index(at) + 1) * wide]
            for at in range(count)
        ],
        axis=1,
    )
    return (states, projected)


def solution(mesh):
    return jax.shard_map(
        shards,
        mesh=mesh,
        in_specs=(
            P(("groups", "tok"), None, None),
            P(("groups", "tok"), None, None),
            P(("groups", "tok"), None),
            P(("groups", "tok"), None),
            P("groups"),
            P(None, "tok"),
        ),
        out_specs=(P(("groups", "tok"), None), P(("groups", "tok"), None)),
        check_vma=False,
    )
```
